512 devices in a mesh: island: 16 (over x, z_lo), fsdp: 32 (over z_hi, y, core).
Axes of the slice: x: 4, y: 8, z: 8 (z_hi: 2, z_lo: 4; z = z_hi * 4 + z_lo), core: 2. Of those that a mesh axis runs over, the one named last changes fastest.
Arguments:
- key_grad: bfloat16 [65536, 512], P(('island', 'fsdp')), may hold values from -0.25 to 0.25
- layer_input: bfloat16 [65536, 8192], P(('island', 'fsdp')), may hold values from -24 to 24
- key_weight: bfloat16 [16, 8192, 512], P('island', 'fsdp'), may hold values from -0.0625 to 0.0625
- outer_frag: float32 [128, 8192], P(None, 'fsdp'), may hold values from -6 to 6
- momentum: float32 [128, 8192], P(None, 'fsdp'), may hold values from -6 to 6
- inner_frag: bfloat16 [2048, 8192], P('island', 'fsdp'), may hold values from -6 to 6
Outputs:
- keys: bfloat16 [65536, 512], P(('island', 'fsdp'))
- weight_grad: float32 [16, 8192, 512], P('island', 'fsdp')
- new_outer: float32 [128, 8192], P(None, 'fsdp')
- new_momentum: float32 [128, 8192], P(None, 'fsdp')
The draws below stay inside these ranges and needn't reach their ends.
All inputs are finite; a program needn't handle non-finite values.
Results may differ from the reference program's by a relative error of at most 0.0065.
Values may be sent and summed in bfloat16 or wider, within the bound.
A program may use at most 64 MiB of HBM per device.

```python
import jax
import jax.numpy as jnp
from jax import lax

D = 8192
TOK_DEV = 128
FRAG_ROWS = 128
E = 512
TOKENS = 65536
N_ISLAND = 16
N_FSDP = 32


def raised(array, rng, source, target, shards_of, factor):
    def block_of(dim):
        return (jnp.arange(array.shape[dim]) // (array.shape[dim] // shards_of)).reshape((-1,) + (1,) * (array.ndim - 1 - dim))

    one_side = jax.random.permutation(rng, shards_of)[block_of(target)]
    far = (block_of(target) + shards_of // 2) % shards_of
    return jnp.where((block_of(source) == one_side) | (block_of(source) == far), factor * array, array)


def block_levels(rng, dims, shards, least, high):
    gain, own = 1.0, jax.random.fold_in(rng, 6)
    for axis_at, blocks in shards:
        steps = jnp.exp(jax.random.uniform(jax.random.fold_in(own, axis_at), (blocks,), jnp.float32, least / len(shards), high / len(shards)))
        gain = gain * jnp.repeat(steps, dims[axis_at] // blocks).reshape([-1 if axis == axis_at else 1 for axis in range(len(dims))])
    return gain


def noise(rng, dims, deviation, limit, split=(), held_as=jnp.bfloat16):
    entries = jax.random.normal(rng, dims, jnp.float32) * deviation
    if len(split) > 0:
        entries = block_levels(rng, dims, split, -0.22, 0.18) * entries
    return jnp.clip(entries, min=-limit, max=limit).astype(held_as)


def heavy_noise(key, extent, deviation, bound, cuts, heavy, held_as=jnp.bfloat16):
    values = deviation * jax.random.normal(key, extent, jnp.float32)
    if cuts:
        values = values * block_levels(key, extent, cuts, -0.22, 0.18)
    return jnp.clip(raised(values, jax.random.fold_in(key, 3), *heavy), -bound, bound).astype(held_as)


def setup_inputs(seed: int = 0) -> dict:
    key_of = jax.random.split(jax.random.key(seed), 7)
    return {
        "key_grad": noise(key_of[0], (TOKENS, E), ((TOK_DEV * N_FSDP) ** -0.5), 0.25, ((0, 512),)),
        "layer_input": heavy_noise(key_of[1], (TOKENS, D), 1.0, 24.0, ((0, 512),), (0, 1, 512, 6.0)),
        "key_weight": noise(key_of[2], (N_ISLAND, D, E), D ** -0.5, 0.0625, ((0, 16), (1, 32))),
        "outer_frag": noise(key_of[3], (FRAG_ROWS, D), 1.0, 6.0, ((1, 32),), jnp.float32),
        "momentum": noise(key_of[4], (FRAG_ROWS, D), 0.5, 6.0, ((1, 32),), jnp.float32),
        "inner_frag": noise(key_of[5], (N_ISLAND * FRAG_ROWS, D), 1.0, 6.0, ((0, 16), (1, 32))),
    }


def replica_step(pieces):
    input_rep, grad_rep, weight_rep = pieces
    keys = jnp.dot(input_rep, weight_rep, preferred_element_type=jnp.float32).astype(jnp.bfloat16)
    input_blocks = input_rep.reshape(N_FSDP, TOK_DEV, D)
    grad_blocks = grad_rep.reshape(N_FSDP, TOK_DEV, E)

    def add_block(total, block):
        input_block, grad_block = block
        term = jnp.dot(input_block.T, grad_block, preferred_element_type=jnp.float32).astype(jnp.bfloat16)
        term = lax.optimization_barrier(term)
        return total + term.astype(jnp.float32), None

    grad, unused = lax.scan(add_block, jnp.zeros((D, E), jnp.float32), (input_blocks, grad_blocks))
    return keys, grad


def reference(key_grad, layer_input, key_weight, outer_frag, momentum, inner_frag):
    input_all = layer_input.reshape(N_ISLAND, TOK_DEV * N_FSDP, D)
    grad_all = key_grad.reshape(N_ISLAND, TOK_DEV * N_FSDP, E)
    keys, weight_grad = lax.map(replica_step, (input_all, grad_all, key_weight))
    keys = keys.reshape(N_ISLAND * TOK_DEV * N_FSDP, E)
    inner = inner_frag.reshape(N_ISLAND, FRAG_ROWS, D).astype(jnp.float32)
    delta = outer_frag[None] - inner
    pseudo = jnp.sum(delta, axis=0) / N_ISLAND
    new_momentum = 0.9 * momentum + pseudo
    new_outer = outer_frag - 0.7 * (pseudo + 0.9 * new_momentum)
    return keys, weight_grad, new_outer, new_momentum
```

```python
import functools

import jax
import jax.numpy as jnp
from jax import lax
from jax.experimental import pallas as pl
from jax.experimental.pallas import tpu as pltpu
from jax.sharding import PartitionSpec as P

MESH = pl.DeviceIdType.MESH
TOK, WIDTH, FEAT, ROWS = 128, 8192, 512, 256
LEFT, RIGHT = 0, 1
FAR, OWN = 0, 1

X0 = 0
DK0 = X0 + 12
WY = DK0 + 6
WC0 = WY + 1
WZ0 = WC0 + 4
GC0 = WZ0 + 2
GZ0 = GC0 + 4
GY = GZ0 + 2
K0 = GY + 1
FX0 = K0 + 6
FZ0 = FX0 + 3
FA0 = FZ0 + 3
FB0 = FA0 + 3
COPIES = FB0 + 3


def dot(a, b):
    return jnp.dot(a, b, preferred_element_type=jnp.float32)


def dot_rows(a, b):
    return lax.dot_general(a, b, (((0,), (0,)), ((), ())), preferred_element_type=jnp.float32)


def kernel(
    dk_ref, x_ref, w_ref, outer_ref, mom_ref, inner_ref,
    keys_ref, grad_ref, new_outer_ref, new_mom_ref,
    xs, dks, ws, part, ksend, krecv, g, gcore, gzs, gzr, gys, gyr,
    fx, acc, fz, pseudo, send, recv, local,
):
    island, f = lax.axis_index("island"), lax.axis_index("fsdp")
    x, zl = island // 4, island % 4
    zh, y, c = f // 16, (f // 2) % 8, f % 2

    def at(dx=0, dzl=0, dzh=0, dy=0, dc=0):
        return (
            ((x + dx) % 4) * 4 + (zl + dzl) % 4,
            ((zh + dzh) % 2) * 16 + ((y + dy + 8) % 8) * 2 + (c + dc) % 2,
        )

    def copy(src, dst, sem, to):
        return pltpu.make_async_remote_copy(
            src_ref=src, dst_ref=dst, send_sem=send.at[sem], recv_sem=recv.at[sem],
            device_id=to, device_id_type=MESH,
        )

    started = []

    def start(src, dst, sem, to):
        moved = copy(src, dst, sem, to)
        moved.start()
        started.append(moved)
        return moved

    def cols(owner, plane):
        return pl.ds(pl.multiple_of(((plane + 2) % 2) * 4096 + ((owner + 8) % 8) * 512, 512), 512)

    def tok(d):
        return pl.ds(d * TOK, TOK)

    mine = pl.ds(pl.multiple_of(c * ROWS, ROWS), ROWS)
    other = pl.ds(pl.multiple_of((1 - c) * ROWS, ROWS), ROWS)
    plane = [zh + 1, zh]

    loads = []
    for role in (LEFT, RIGHT):
        loads.append((dk_ref, dks.at[role, tok(0)]))
        for p in (FAR, OWN):
            loads.append((x_ref.at[:, cols(y - role, plane[p])], xs.at[p, role, tok(0)]))
    loads.append((w_ref.at[0], ws.at[OWN, LEFT, mine]))
    loads = [pltpu.make_async_copy(s, d, local.at[k]) for k, (s, d) in enumerate(loads)]
    for load in loads:
        load.start()

    barrier = pltpu.get_barrier_semaphore()
    partners = [at(dy=d) for d in (1, -1, 2, -2, 3, -3)]
    partners += [at(dc=1), at(dzh=1)]
    partners += [at(dx=k) for k in (1, 2, 3)] + [at(dzl=k) for k in (1, 2, 3)]
    for partner in partners:
        pl.semaphore_signal(barrier, inc=1, device_id=partner, device_id_type=MESH)
    pl.semaphore_wait(barrier, len(partners))

    sign = (1, -1)

    def x_copy(p, role, d):
        owner = y + d if role == LEFT else y - d - 1
        return (
            x_ref.at[:, cols(owner, plane[p])], xs.at[p, role, tok(d)],
            X0 + p * 6 + role * 3 + d - 1, at(dy=sign[role] * d),
        )

    def dk_copy(role, d):
        src = dk_ref if d == 1 else dks.at[role, tok(d - 1)]
        return src, dks.at[role, tok(d)], DK0 + role * 3 + d - 1, at(dy=sign[role])

    def w_core(p, role):
        src = w_ref.at[0] if (p, role) == (OWN, LEFT) else ws.at[p, role, mine]
        return src, ws.at[p, role, mine], WC0 + p * 2 + role, at(dc=1)

    def w_far(role):
        src = w_ref.at[0] if role == LEFT else ws.at[OWN, role, mine]
        return src, ws.at[FAR, role, mine], WZ0 + role, at(dzh=1)

    w_next = (w_ref.at[0], ws.at[OWN, RIGHT, mine], WY, at(dy=1))

    def k_copy(role, d):
        return ksend.at[role, d - 1], krecv.at[role, d - 1], K0 + role * 3 + d - 1, at(dy=-sign[role])

    def arrived(args):
        copy(*args).wait_recv()

    start(*dk_copy(LEFT, 1))
    start(*dk_copy(RIGHT, 1))
    start(*w_next)
    start(*w_far(LEFT))
    start(*w_core(OWN, LEFT))
    for k in (1, 2, 3):
        peer = (x + k) % 4
        start(inner_ref.at[pl.ds(pl.multiple_of(peer * 32, 32), 32)], fx.at[k - 1], FX0 + k - 1, at(dx=k))
    for d in (3, 2, 1):
        for role in (LEFT, RIGHT):
            start(*x_copy(FAR, role, d))

    for role in (LEFT, RIGHT):
        arrived(dk_copy(role, 1))
        start(*dk_copy(role, 2))
    arrived(w_next)
    start(*w_far(RIGHT))
    start(*w_core(OWN, RIGHT))
    for role in (LEFT, RIGHT):
        arrived(dk_copy(role, 2))
        start(*dk_copy(role, 3))
    for d in (3, 2, 1):
        for role in (LEFT, RIGHT):
            start(*x_copy(OWN, role, d))

    block = pl.ds(pl.multiple_of(x * 32, 32), 32)
    eight = pl.ds(pl.multiple_of(x * 32 + zl * 8, 8), 8)
    outer_block = outer_ref[block, :]
    total = outer_block - inner_ref[block, :].astype(jnp.float32)
    for k in (1, 2, 3):
        copy(fx.at[k - 1], fx.at[k - 1], FX0 + k - 1, at(dx=k)).wait_recv()
        total = total + (outer_block - fx[k - 1].astype(jnp.float32))
    acc[...] = total
    for k in (1, 2, 3):
        peer = (zl + k) % 4
        start(acc.at[pl.ds(pl.multiple_of(peer * 8, 8), 8)], fz.at[k - 1], FZ0 + k - 1, at(dzl=k))

    for load in loads:
        load.wait()
    arrived(w_far(LEFT))
    start(*w_core(FAR, LEFT))

    for role in (LEFT, RIGHT):
        for d in (3, 2, 1):
            arrived(x_copy(FAR, role, d))
        arrived(dk_copy(role, 3))
        g[FAR, role] = dot_rows(xs[FAR, role], dks[role])
        start(g.at[FAR, role, other], gcore.at[FAR, role], GC0 + FAR * 2 + role, at(dc=1))

    total = acc[pl.ds(pl.multiple_of(zl * 8, 8), 8), :]
    for k in (1, 2, 3):
        copy(fz.at[k - 1], fz.at[k - 1], FZ0 + k - 1, at(dzl=k)).wait_recv()
        total = total + fz[k - 1]
    pseudo[eight, :] = total / 16
    for k in (1, 2, 3):
        start(pseudo.at[eight], pseudo.at[eight], FA0 + k - 1, at(dzl=k))

    for role in (RIGHT, LEFT):
        copy(gcore.at[FAR, role], gcore.at[FAR, role], GC0 + FAR * 2 + role, at(dc=1)).wait_recv()
        gzs[role] = (g[FAR, role, mine, :] + gcore[FAR, role]).astype(jnp.bfloat16)
        start(gzs.at[role], gzr.at[role], GZ0 + role, at(dzh=1))

    for k in (1, 2, 3):
        came = pl.ds(pl.multiple_of(x * 32 + ((zl + 4 - k) % 4) * 8, 8), 8)
        copy(pseudo.at[came], pseudo.at[came], FA0 + k - 1, at(dzl=k)).wait_recv()
    for k in (1, 2, 3):
        start(pseudo.at[block], pseudo.at[block], FB0 + k - 1, at(dx=k))

    arrived(w_far(RIGHT))
    start(*w_core(FAR, RIGHT))
    for role in (LEFT, RIGHT):
        for p in (FAR, OWN):
            arrived(w_core(p, role))
    for role in (LEFT, RIGHT):
        part[role] = dot(xs[FAR, role], ws[FAR, role])

    for d in (3, 2, 1):
        for role in (LEFT, RIGHT):
            arrived(x_copy(OWN, role, d))
            value = part[role, tok(d), :] + dot(xs[OWN, role, tok(d), :], ws[OWN, role])
            if d < 3:
                arrived(k_copy(role, d + 1))
                value = value + krecv[role, d].astype(jnp.float32)
            ksend[role, d - 1] = value.astype(jnp.bfloat16)
            start(*k_copy(role, d))

    for role in (RIGHT, LEFT):
        g[OWN, role] = dot_rows(xs[OWN, role], dks[role])
        start(g.at[OWN, role, other], gcore.at[OWN, role], GC0 + OWN * 2 + role, at(dc=1))

    def own_total(role):
        copy(gcore.at[OWN, role], gcore.at[OWN, role], GC0 + OWN * 2 + role, at(dc=1)).wait_recv()
        copy(gzs.at[role], gzr.at[role], GZ0 + role, at(dzh=1)).wait_recv()
        return g[OWN, role, mine, :] + gcore[OWN, role] + gzr[role].astype(jnp.float32)

    gys[...] = own_total(RIGHT).astype(jnp.bfloat16)
    start(gys, gyr, GY, at(dy=-1))
    g[OWN, LEFT, mine, :] = own_total(LEFT)

    for k in (1, 2, 3):
        came = pl.ds(pl.multiple_of(((x + 4 - k) % 4) * 32, 32), 32)
        copy(pseudo.at[came], pseudo.at[came], FB0 + k - 1, at(dx=k)).wait_recv()
    new_mom = 0.9 * mom_ref[...] + pseudo[...]
    new_mom_ref[...] = new_mom
    new_outer_ref[...] = outer_ref[...] - 0.7 * (pseudo[...] + 0.9 * new_mom)

    own_keys = part[LEFT, tok(0), :] + part[RIGHT, tok(0), :]
    for role in (LEFT, RIGHT):
        own_keys = own_keys + dot(xs[OWN, role, tok(0), :], ws[OWN, role])
    for role in (LEFT, RIGHT):
        arrived(k_copy(role, 1))
        own_keys = own_keys + krecv[role, 0].astype(jnp.float32)
    keys_ref[...] = own_keys.astype(jnp.bfloat16)

    copy(gys, gyr, GY, at(dy=-1)).wait_recv()
    grad_ref[...] = g[OWN, LEFT, mine, :] + gyr[...].astype(jnp.float32)

    for moved in started:
        moved.wait_send()


def body(key_grad, layer_input, key_weight, outer_frag, momentum, inner_frag):
    whole = pl.BlockSpec(memory_space=pltpu.VMEM)
    bf16, f32 = jnp.bfloat16, jnp.float32
    keys, grad, new_outer, new_momentum = pl.pallas_call(
        kernel,
        name="exchange",
        out_shape=(
            jax.ShapeDtypeStruct((TOK, FEAT), bf16),
            jax.ShapeDtypeStruct((ROWS, FEAT), f32),
            jax.ShapeDtypeStruct(outer_frag.shape, f32),
            jax.ShapeDtypeStruct(outer_frag.shape, f32),
        ),
        in_specs=[pl.BlockSpec(memory_space=pl.ANY)] * 3 + [whole] * 3,
        out_specs=(whole,) * 4,
        scratch_shapes=[
            pltpu.VMEM((2, 2, 4 * TOK, 512), bf16),
            pltpu.VMEM((2, 4 * TOK, FEAT), bf16),
            pltpu.VMEM((2, 2, 2 * ROWS, FEAT), bf16),
            pltpu.VMEM((2, 4 * TOK, FEAT), f32),
            pltpu.VMEM((2, 3, TOK, FEAT), bf16),
            pltpu.VMEM((2, 3, TOK, FEAT), bf16),
            pltpu.VMEM((2, 2, 2 * ROWS, FEAT), f32),
            pltpu.VMEM((2, 2, ROWS, FEAT), f32),
            pltpu.VMEM((2, ROWS, FEAT), bf16),
            pltpu.VMEM((2, ROWS, FEAT), bf16),
            pltpu.VMEM((ROWS, FEAT), bf16),
            pltpu.VMEM((ROWS, FEAT), bf16),
            pltpu.VMEM((3, 32, 256), bf16),
            pltpu.VMEM((32, 256), f32),
            pltpu.VMEM((3, 8, 256), f32),
            pltpu.VMEM((128, 256), f32),
            pltpu.SemaphoreType.DMA((COPIES,)),
            pltpu.SemaphoreType.DMA((COPIES,)),
            pltpu.SemaphoreType.DMA((7,)),
        ],
        compiler_params=pltpu.CompilerParams(
            collective_id=0, has_side_effects=True, vmem_limit_bytes=40 << 20
        ),
    )(key_grad, layer_input, key_weight, outer_frag, momentum, inner_frag)
    return keys, grad[None], new_outer, new_momentum


def solution(mesh):
    placed = (
        P(("island", "fsdp"), None),
        P(("island", "fsdp"), None),
        P("island", "fsdp", None),
        P(None, "fsdp"),
        P(None, "fsdp"),
        P("island", "fsdp"),
    )
    return jax.shard_map(
        body,
        mesh=mesh,
        in_specs=placed,
        out_specs=(
            P(("island", "fsdp"), None),
            P("island", "fsdp", None),
            P(None, "fsdp"),
            P(None, "fsdp"),
        ),
        check_vma=False,
    )
```

```python
import functools

import jax
import jax.numpy as jnp
from jax import lax
from jax.experimental import pallas as pl
from jax.experimental.pallas import tpu as pltpu
from jax.sharding import PartitionSpec as P

MESH = pl.DeviceIdType.MESH
TOK, WIDTH, FEAT, ROWS = 128, 8192, 512, 256
LEFT, RIGHT = 0, 1
FAR, OWN = 0, 1
VMEM_MB = 56

X0 = 0
DK0 = X0 + 12
WY = DK0 + 6
WC0 = WY + 1
WZ0 = WC0 + 4
GC0 = WZ0 + 2
GZ0 = GC0 + 4
GY = GZ0 + 2
K0 = GY + 1
FX0 = K0 + 6
FZ0 = FX0 + 3
FA0 = FZ0 + 3
FB0 = FA0 + 3
COPIES = FB0 + 3


def dot(a, b):
    return jnp.dot(a, b, preferred_element_type=jnp.float32)


def dot_rows(a, b):
    return lax.dot_general(a, b, (((0,), (0,)), ((), ())), preferred_element_type=jnp.float32)


def kernel(
    dk_ref, x_ref, w_ref, outer_hbm, mom_hbm, inner_hbm,
    keys_ref, grad_ref, new_outer_ref, new_mom_ref,
    xs, dks, ws, part, ksend, krecv, g, gcore, gzs, gzr, gys, gyr,
    outer_ref, mom_ref, inner_ref, fx, acc, fz, pseudo, send, recv, local,
):
    island, f = lax.axis_index("island"), lax.axis_index("fsdp")
    x, zl = island // 4, island % 4
    zh, y, c = f // 16, (f // 2) % 8, f % 2

    def at(dx=0, dzl=0, dzh=0, dy=0, dc=0):
        return (
            ((x + dx) % 4) * 4 + (zl + dzl) % 4,
            ((zh + dzh) % 2) * 16 + ((y + dy + 8) % 8) * 2 + (c + dc) % 2,
        )

    def copy(src, dst, sem, to):
        return pltpu.make_async_remote_copy(
            src_ref=src, dst_ref=dst, send_sem=send.at[sem], recv_sem=recv.at[sem],
            device_id=to, device_id_type=MESH,
        )

    started = []

    def start(src, dst, sem, to):
        moved = copy(src, dst, sem, to)
        moved.start()
        started.append(moved)
        return moved

    def cols(owner, plane):
        return pl.ds(pl.multiple_of(((plane + 2) % 2) * 4096 + ((owner + 8) % 8) * 512, 512), 512)

    def tok(d):
        return pl.ds(d * TOK, TOK)

    mine = pl.ds(pl.multiple_of(c * ROWS, ROWS), ROWS)
    other = pl.ds(pl.multiple_of((1 - c) * ROWS, ROWS), ROWS)
    plane = [zh + 1, zh]

    loads = []
    for role in (LEFT, RIGHT):
        loads.append((dk_ref, dks.at[role, tok(0)]))
        for p in (FAR, OWN):
            loads.append((x_ref.at[:, cols(y - role, plane[p])], xs.at[p, role, tok(0)]))
    loads.append((w_ref.at[0], ws.at[OWN, LEFT, mine]))
    loads += [(inner_hbm, inner_ref), (outer_hbm, outer_ref), (mom_hbm, mom_ref)]
    loads = [pltpu.make_async_copy(s, d, local.at[k]) for k, (s, d) in enumerate(loads)]
    for load in loads:
        load.start()

    barrier = pltpu.get_barrier_semaphore()
    partners = [at(dy=d) for d in (1, -1, 2, -2, 3, -3)]
    partners += [at(dc=1), at(dzh=1)]
    partners += [at(dx=k) for k in (1, 2, 3)] + [at(dzl=k) for k in (1, 2, 3)]
    for partner in partners:
        pl.semaphore_signal(barrier, inc=1, device_id=partner, device_id_type=MESH)
    pl.semaphore_wait(barrier, len(partners))

    sign = (1, -1)

    def x_copy(p, role, d):
        owner = y + d if role == LEFT else y - d - 1
        return (
            x_ref.at[:, cols(owner, plane[p])], xs.at[p, role, tok(d)],
            X0 + p * 6 + role * 3 + d - 1, at(dy=sign[role] * d),
        )

    def dk_copy(role, d):
        src = dk_ref if d == 1 else dks.at[role, tok(d - 1)]
        return src, dks.at[role, tok(d)], DK0 + role * 3 + d - 1, at(dy=sign[role])

    def w_core(p, role):
        src = w_ref.at[0] if (p, role) == (OWN, LEFT) else ws.at[p, role, mine]
        return src, ws.at[p, role, mine], WC0 + p * 2 + role, at(dc=1)

    def w_far(role):
        src = w_ref.at[0] if role == LEFT else ws.at[OWN, role, mine]
        return src, ws.at[FAR, role, mine], WZ0 + role, at(dzh=1)

    w_next = (w_ref.at[0], ws.at[OWN, RIGHT, mine], WY, at(dy=1))

    def k_copy(role, d):
        return ksend.at[role, d - 1], krecv.at[role, d - 1], K0 + role * 3 + d - 1, at(dy=-sign[role])

    def arrived(args):
        copy(*args).wait_recv()

    order = [(p, d) for p in (FAR, OWN) for d in (3, 2, 1)]
    under_way, left = ([], []), []

    def send_x(role):
        sent = under_way[role]
        if len(sent) >= 3:
            sent[-3].wait_send()
            left.append(id(sent[-3]))
        p, d = order[len(sent)]
        sent.append(start(*x_copy(p, role, d)))

    both = (RIGHT, LEFT)
    for role in both:
        start(*dk_copy(role, 1))
    start(*w_next)
    start(*w_far(LEFT))
    start(*w_core(OWN, LEFT))
    for k in (1, 2, 3):
        peer = (x + k) % 4
        start(inner_hbm.at[pl.ds(pl.multiple_of(peer * 32, 32), 32)], fx.at[k - 1], FX0 + k - 1, at(dx=k))
    for _ in range(3):
        for role in both:
            send_x(role)

    for role in both:
        arrived(dk_copy(role, 1))
        start(*dk_copy(role, 2))
    arrived(w_next)
    start(*w_far(RIGHT))
    start(*w_core(OWN, RIGHT))
    for role in both:
        arrived(dk_copy(role, 2))
        start(*dk_copy(role, 3))

    for load in loads:
        load.wait()

    block = pl.ds(pl.multiple_of(x * 32, 32), 32)
    eight = pl.ds(pl.multiple_of(x * 32 + zl * 8, 8), 8)
    outer_block = outer_ref[block, :]
    total = outer_block - inner_ref[block, :].astype(jnp.float32)
    for k in (1, 2, 3):
        arrived((fx.at[k - 1], fx.at[k - 1], FX0 + k - 1, at(dx=k)))
        total = total + (outer_block - fx[k - 1].astype(jnp.float32))
    acc[...] = total
    for k in (1, 2, 3):
        peer = (zl + k) % 4
        start(acc.at[pl.ds(pl.multiple_of(peer * 8, 8), 8)], fz.at[k - 1], FZ0 + k - 1, at(dzl=k))

    for role in both:
        send_x(role)

    total = acc[pl.ds(pl.multiple_of(zl * 8, 8), 8), :]
    for k in (1, 2, 3):
        arrived((fz.at[k - 1], fz.at[k - 1], FZ0 + k - 1, at(dzl=k)))
        total = total + fz[k - 1]
    pseudo[eight, :] = total / 16
    for k in (1, 2, 3):
        start(pseudo.at[eight], pseudo.at[eight], FA0 + k - 1, at(dzl=k))

    arrived(w_far(LEFT))
    start(*w_core(FAR, LEFT))

    for role in both:
        send_x(role)

    def g_core(p, role):
        return g.at[p, role, other], gcore.at[p, role], GC0 + p * 2 + role, at(dc=1)

    def far_product(role):
        for d in (3, 2, 1):
            arrived(x_copy(FAR, role, d))
        arrived(dk_copy(role, 3))
        g[FAR, role] = dot_rows(xs[FAR, role], dks[role])
        start(*g_core(FAR, role))

    def far_total(role):
        arrived(g_core(FAR, role))
        gzs[role] = (g[FAR, role, mine, :] + gcore[FAR, role]).astype(jnp.bfloat16)
        start(gzs.at[role], gzr.at[role], GZ0 + role, at(dzh=1))

    far_product(RIGHT)
    send_x(RIGHT)
    far_total(RIGHT)
    far_product(LEFT)
    send_x(LEFT)
    far_total(LEFT)

    for k in (1, 2, 3):
        came = pl.ds(pl.multiple_of(x * 32 + ((zl + 4 - k) % 4) * 8, 8), 8)
        arrived((pseudo.at[came], pseudo.at[came], FA0 + k - 1, at(dzl=k)))
    for k in (1, 2, 3):
        start(pseudo.at[block], pseudo.at[block], FB0 + k - 1, at(dx=k))

    arrived(w_far(RIGHT))
    start(*w_core(FAR, RIGHT))
    for role in both:
        for p in (FAR, OWN):
            arrived(w_core(p, role))
    for role in both:
        part[role] = dot(xs[FAR, role], ws[FAR, role])

    def pass_keys(role, d, here=False):
        if not here:
            arrived(x_copy(OWN, role, d))
        value = part[role, tok(d), :] + dot(xs[OWN, role, tok(d), :], ws[OWN, role])
        if d < 3:
            arrived(k_copy(role, d + 1))
            value = value + krecv[role, d].astype(jnp.float32)
        ksend[role, d - 1] = value.astype(jnp.bfloat16)
        start(*k_copy(role, d))

    soon, late = pl.ds(0, 2 * TOK), pl.ds(2 * TOK, 2 * TOK)

    def own_late(role):
        g[OWN, role] = dot_rows(xs[OWN, role, late, :], dks[role, late, :])

    def own_soon(role):
        g[OWN, role] += dot_rows(xs[OWN, role, soon, :], dks[role, soon, :])
        start(*g_core(OWN, role))

    def own_total(role):
        arrived(g_core(OWN, role))
        arrived((gzs.at[role], gzr.at[role], GZ0 + role, at(dzh=1)))
        return g[OWN, role, mine, :] + gcore[OWN, role] + gzr[role].astype(jnp.float32)

    pass_keys(RIGHT, 3)
    pass_keys(LEFT, 3)
    pass_keys(RIGHT, 2)
    own_late(RIGHT)
    pass_keys(LEFT, 2)
    own_late(LEFT)
    arrived(x_copy(OWN, RIGHT, 1))
    own_soon(RIGHT)
    pass_keys(RIGHT, 1, here=True)
    gys[...] = own_total(RIGHT).astype(jnp.bfloat16)
    start(gys, gyr, GY, at(dy=-1))
    pass_keys(LEFT, 1)
    own_soon(LEFT)

    own_keys = part[LEFT, tok(0), :] + part[RIGHT, tok(0), :]
    for role in both:
        own_keys = own_keys + dot(xs[OWN, role, tok(0), :], ws[OWN, role])
    part[LEFT, tok(0), :] = own_keys

    for k in (1, 2, 3):
        came = pl.ds(pl.multiple_of(((x + 4 - k) % 4) * 32, 32), 32)
        arrived((pseudo.at[came], pseudo.at[came], FB0 + k - 1, at(dx=k)))
    new_mom = 0.9 * mom_ref[...] + pseudo[...]
    new_mom_ref[...] = new_mom
    new_outer_ref[...] = outer_ref[...] - 0.7 * (pseudo[...] + 0.9 * new_mom)

    g[OWN, LEFT, mine, :] = own_total(LEFT)

    own_keys = part[LEFT, tok(0), :]
    for role in both:
        arrived(k_copy(role, 1))
        own_keys = own_keys + krecv[role, 0].astype(jnp.float32)
    keys_ref[...] = own_keys.astype(jnp.bfloat16)

    arrived((gys, gyr, GY, at(dy=-1)))
    grad_ref[...] = g[OWN, LEFT, mine, :] + gyr[...].astype(jnp.float32)

    for moved in started:
        if id(moved) not in left:
            moved.wait_send()


def finish(*refs):
    for k in range(4):
        refs[4 + k][...] = refs[k][...]


def body(key_grad, layer_input, key_weight, outer_frag, momentum, inner_frag):
    whole = pl.BlockSpec(memory_space=pltpu.VMEM)
    bf16, f32 = jnp.bfloat16, jnp.float32
    results = pl.pallas_call(
        kernel,
        name="exchange",
        out_shape=(
            jax.ShapeDtypeStruct((TOK, FEAT), bf16),
            jax.ShapeDtypeStruct((ROWS, FEAT), f32),
            jax.ShapeDtypeStruct(outer_frag.shape, f32),
            jax.ShapeDtypeStruct(outer_frag.shape, f32),
        ),
        in_specs=[pl.BlockSpec(memory_space=pltpu.HBM)] * 6,
        out_specs=(whole,) * 4,
        scratch_shapes=[
            pltpu.VMEM((2, 2, 4 * TOK, 512), bf16),
            pltpu.VMEM((2, 4 * TOK, FEAT), bf16),
            pltpu.VMEM((2, 2, 2 * ROWS, FEAT), bf16),
            pltpu.VMEM((2, 4 * TOK, FEAT), f32),
            pltpu.VMEM((2, 3, TOK, FEAT), bf16),
            pltpu.VMEM((2, 3, TOK, FEAT), bf16),
            pltpu.VMEM((2, 2, 2 * ROWS, FEAT), f32),
            pltpu.VMEM((2, 2, ROWS, FEAT), f32),
            pltpu.VMEM((2, ROWS, FEAT), bf16),
            pltpu.VMEM((2, ROWS, FEAT), bf16),
            pltpu.VMEM((ROWS, FEAT), bf16),
            pltpu.VMEM((ROWS, FEAT), bf16),
            pltpu.VMEM((128, 256), f32),
            pltpu.VMEM((128, 256), f32),
            pltpu.VMEM((128, 256), bf16),
            pltpu.VMEM((3, 32, 256), bf16),
            pltpu.VMEM((32, 256), f32),
            pltpu.VMEM((3, 8, 256), f32),
            pltpu.VMEM((128, 256), f32),
            pltpu.SemaphoreType.DMA((COPIES,)),
            pltpu.SemaphoreType.DMA((COPIES,)),
            pltpu.SemaphoreType.DMA((10,)),
        ],
        compiler_params=pltpu.CompilerParams(
            collective_id=0, has_side_effects=True, vmem_limit_bytes=VMEM_MB << 20
        ),
    )(key_grad, layer_input, key_weight, outer_frag, momentum, inner_frag)
    keys, grad, new_outer, new_momentum = pl.pallas_call(
        finish,
        name="finish",
        out_shape=[jax.ShapeDtypeStruct(r.shape, r.dtype) for r in results],
        in_specs=[whole] * 4,
        out_specs=[whole] * 4,
    )(*results)
    return keys, grad[None], new_outer, new_momentum


def solution(mesh):
    placed = (
        P(("island", "fsdp"), None),
        P(("island", "fsdp"), None),
        P("island", "fsdp", None),
        P(None, "fsdp"),
        P(None, "fsdp"),
        P("island", "fsdp"),
    )
    return jax.shard_map(
        body,
        mesh=mesh,
        in_specs=placed,
        out_specs=(
            P(("island", "fsdp"), None),
            P("island", "fsdp", None),
            P(None, "fsdp"),
            P(None, "fsdp"),
        ),
        check_vma=False,
    )
```

```python
import functools

import jax
import jax.numpy as jnp
from jax import lax
from jax.experimental import pallas as pl
from jax.experimental.pallas import tpu as pltpu
from jax.sharding import PartitionSpec as P

MESH = pl.DeviceIdType.MESH
TOK, WIDTH, FEAT, ROWS = 128, 8192, 512, 256
LEFT, RIGHT = 0, 1
FAR, OWN = 0, 1
VMEM_MB = 40
FINISH_KB = 53248
PLAN = ((1, 1, 1, 1, 1, 1, 1, 1, 1, 1), (1, 1, 1, 1, 1, 1, 1, 1, 1, 1))
DEPTH = (2, 2)
ORDER = ('a3', 'a2', 'a1', 'o3', 'b3', 'b2', 'b1', 'o2', 'o1')

X0 = 0
DK0 = X0 + 18
WY = DK0 + 6
WC0 = WY + 1
WZ0 = WC0 + 4
GC0 = WZ0 + 2
GZ0 = GC0 + 4
GY = GZ0 + 2
K0 = GY + 1
FX0 = K0 + 6
FZ0 = FX0 + 3
FA0 = FZ0 + 3
FB0 = FA0 + 3
COPIES = FB0 + 3


def dot(a, b):
    return jnp.dot(a, b, preferred_element_type=jnp.float32)


def dot_rows(a, b):
    return lax.dot_general(a, b, (((0,), (0,)), ((), ())), preferred_element_type=jnp.float32)


def kernel(
    dk_ref, x_ref, w_ref, outer_hbm, mom_hbm, inner_hbm,
    keys_ref, grad_ref, new_outer_ref, new_mom_ref,
    xs, dks, ws, part, ksend, krecv, g, gcore, gzs, gzr, gys, gyr,
    outer_ref, mom_ref, inner_ref, fx, acc, fz, pseudo, send, recv, local, entered,
):
    island, f = lax.axis_index("island"), lax.axis_index("fsdp")
    x, zl = island // 4, island % 4
    zh, y, c = f // 16, (f // 2) % 8, f % 2

    def at(dx=0, dzl=0, dzh=0, dy=0, dc=0):
        return (
            ((x + dx) % 4) * 4 + (zl + dzl) % 4,
            ((zh + dzh) % 2) * 16 + ((y + dy + 8) % 8) * 2 + (c + dc) % 2,
        )

    def copy(src, dst, sem, to):
        return pltpu.make_async_remote_copy(
            src_ref=src, dst_ref=dst, send_sem=send.at[sem], recv_sem=recv.at[sem],
            device_id=to, device_id_type=MESH,
        )

    started = []

    def start(src, dst, sem, to):
        moved = copy(src, dst, sem, to)
        moved.start()
        started.append(moved)
        return moved

    def cols(owner, plane, h=None):
        first = ((plane + 2) % 2) * 4096 + ((owner + 8) % 8) * 512
        if h is None:
            return pl.ds(pl.multiple_of(first, 512), 512)
        return pl.ds(pl.multiple_of(first + h * 256, 256), 256)

    def part_cols(h):
        return pl.ds(0, 512) if h is None else pl.ds(h * 256, 256)

    def tok(d):
        return pl.ds(d * TOK, TOK)

    mine = pl.ds(pl.multiple_of(c * ROWS, ROWS), ROWS)
    other = pl.ds(pl.multiple_of((1 - c) * ROWS, ROWS), ROWS)
    plane = [zh + 1, zh]

    loads = []
    for role in (LEFT, RIGHT):
        loads.append((dk_ref, dks.at[role, tok(0)]))
        for p in (FAR, OWN):
            loads.append((x_ref.at[:, cols(y - role, plane[p])], xs.at[p, role, tok(0)]))
    loads.append((w_ref.at[0], ws.at[OWN, LEFT, mine]))
    loads += [(inner_hbm, inner_ref), (outer_hbm, outer_ref), (mom_hbm, mom_ref)]
    loads = [pltpu.make_async_copy(s, d, local.at[k]) for k, (s, d) in enumerate(loads)]
    for load in loads:
        load.start()

    barrier = pltpu.get_barrier_semaphore()

    def tell(semaphore, partner):
        pl.semaphore_signal(semaphore, inc=1, device_id=partner, device_id_type=MESH)

    level = [at(dy=d) for d in (1, -1, 2, -2, 3, -3)] + [at(dc=1)] + [at(dx=k) for k in (1, 2, 3)]
    upright = [(at(dzh=1), zh == 0)] + [(at(dzl=k), zl + k < 4) for k in (1, 2, 3)]
    for partner in level:
        tell(barrier, partner)
    for partner, is_higher in upright:
        pl.when(is_higher)(functools.partial(tell, barrier, partner))
    pl.semaphore_wait(barrier, len(level) + zh + zl)
    for partner, is_higher in upright:
        pl.when(jnp.logical_not(is_higher))(functools.partial(tell, entered.at[0 if partner is upright[0][0] else 1], partner))

    sign = (1, -1)

    def x_copy(p, role, d, h):
        owner = y + d if role == LEFT else y - d - 1
        return (
            x_ref.at[:, cols(owner, plane[p], h)], xs.at[p, role, tok(d), part_cols(h)],
            X0 + (2 * p + (h or 0)) * 6 + role * 3 + d - 1, at(dy=sign[role] * d),
        )

    def dk_copy(role, d):
        src = dk_ref if d == 1 else dks.at[role, tok(d - 1)]
        return src, dks.at[role, tok(d)], DK0 + role * 3 + d - 1, at(dy=sign[role])

    def w_core(p, role):
        src = w_ref.at[0] if (p, role) == (OWN, LEFT) else ws.at[p, role, mine]
        return src, ws.at[p, role, mine], WC0 + p * 2 + role, at(dc=1)

    def w_far(role):
        src = w_ref.at[0] if role == LEFT else ws.at[OWN, role, mine]
        return src, ws.at[FAR, role, mine], WZ0 + role, at(dzh=1)

    w_next = (w_ref.at[0], ws.at[OWN, RIGHT, mine], WY, at(dy=1))

    def k_copy(role, d):
        return ksend.at[role, d - 1], krecv.at[role, d - 1], K0 + role * 3 + d - 1, at(dy=-sign[role])

    seen = set()

    def arrived(args):
        if args[2] not in seen:
            seen.add(args[2])
            copy(*args).wait_recv()

    kinds = {"a": (FAR, 0), "b": (FAR, 1), "o": (OWN, None)}
    order = [(kinds[e[0]][0], int(e[1]), kinds[e[0]][1]) for e in ORDER]
    under_way, left = ([], []), []
    both = (RIGHT, LEFT)

    def send_x(role):
        sent, depth = under_way[role], DEPTH[role]
        if len(sent) == len(order):
            return
        if len(sent) >= depth:
            sent[-depth].wait_send()
            left.append(id(sent[-depth]))
        p, d, h = order[len(sent)]
        sent.append(start(*x_copy(p, role, d, h)))

    def send_both(site):
        for role in both:
            for _ in range(PLAN[role][site]):
                send_x(role)

    for role in both:
        start(*dk_copy(role, 1))
    start(*w_next)
    first_far = copy(*w_far(LEFT))
    started.append(first_far)
    pl.when(zh == 1)(first_far.start)
    start(*w_core(OWN, LEFT))
    for k in (1, 2, 3):
        peer = (x + k) % 4
        start(inner_hbm.at[pl.ds(pl.multiple_of(peer * 32, 32), 32)], fx.at[k - 1], FX0 + k - 1, at(dx=k))
    send_both(0)

    for role in both:
        arrived(dk_copy(role, 1))
        start(*dk_copy(role, 2))
    send_both(1)

    @pl.when(zh == 0)
    def _():
        pl.semaphore_wait(entered.at[0], 1)
        first_far.start()

    arrived(w_next)
    start(*w_far(RIGHT))
    start(*w_core(OWN, RIGHT))
    for role in both:
        arrived(dk_copy(role, 2))
        start(*dk_copy(role, 3))
    send_both(2)

    for load in loads:
        load.wait()

    block = pl.ds(pl.multiple_of(x * 32, 32), 32)
    eight = pl.ds(pl.multiple_of(x * 32 + zl * 8, 8), 8)
    outer_block = outer_ref[block, :]
    total = outer_block - inner_ref[block, :].astype(jnp.float32)
    for k in (1, 2, 3):
        arrived((fx.at[k - 1], fx.at[k - 1], FX0 + k - 1, at(dx=k)))
        total = total + (outer_block - fx[k - 1].astype(jnp.float32))
    acc[...] = total

    @pl.when(zl < 3)
    def _():
        pl.semaphore_wait(entered.at[1], 3 - zl)

    for k in (1, 2, 3):
        peer = (zl + k) % 4
        start(acc.at[pl.ds(pl.multiple_of(peer * 8, 8), 8)], fz.at[k - 1], FZ0 + k - 1, at(dzl=k))

    send_both(3)

    total = acc[pl.ds(pl.multiple_of(zl * 8, 8), 8), :]
    for k in (1, 2, 3):
        arrived((fz.at[k - 1], fz.at[k - 1], FZ0 + k - 1, at(dzl=k)))
        total = total + fz[k - 1]
    pseudo[eight, :] = total / 16
    for k in (1, 2, 3):
        start(pseudo.at[eight], pseudo.at[eight], FA0 + k - 1, at(dzl=k))

    arrived(w_far(LEFT))
    start(*w_core(FAR, LEFT))

    send_both(4)

    def g_core(p, role):
        return g.at[p, role, other], gcore.at[p, role], GC0 + p * 2 + role, at(dc=1)

    def far_product(role, h):
        for d in (3, 2, 1):
            arrived(x_copy(FAR, role, d, h))
        if h == 0:
            arrived(dk_copy(role, 3))
        g[FAR, role, pl.ds(h * 256, 256), :] = dot_rows(xs[FAR, role, :, part_cols(h)], dks[role])
        moved = copy(*g_core(FAR, role))
        pl.when(c != h)(moved.start)

    def far_total(role, h):
        came = copy(*g_core(FAR, role))
        moved = copy(gzs.at[role], gzr.at[role], GZ0 + role, at(dzh=1))

        @pl.when(c == h)
        def _():
            came.wait_recv()
            gzs[role] = (g[FAR, role, pl.ds(h * 256, 256), :] + gcore[FAR, role]).astype(jnp.bfloat16)
            moved.start()

    for role in both:
        far_product(role, 0)
    for role in both:
        far_total(role, 0)
    send_both(5)

    for k in (1, 2, 3):
        came = pl.ds(pl.multiple_of(x * 32 + ((zl + 4 - k) % 4) * 8, 8), 8)
        arrived((pseudo.at[came], pseudo.at[came], FA0 + k - 1, at(dzl=k)))
    for k in (1, 2, 3):
        start(pseudo.at[block], pseudo.at[block], FB0 + k - 1, at(dx=k))
    arrived(w_far(RIGHT))
    start(*w_core(FAR, RIGHT))

    send_both(6)
    for role in both:
        for p in (FAR, OWN):
            arrived(w_core(p, role))

    def keys_part(role, d):
        return dot(xs[FAR, role, tok(d), :], ws[FAR, role]) + dot(xs[OWN, role, tok(d), :], ws[OWN, role])

    def pass_keys(role, d):
        arrived(x_copy(FAR, role, d, 0))
        arrived(x_copy(FAR, role, d, 1))
        arrived(x_copy(OWN, role, d, None))
        value = keys_part(role, d)
        if d < 3:
            arrived(k_copy(role, d + 1))
            value = value + krecv[role, d].astype(jnp.float32)
        ksend[role, d - 1] = value.astype(jnp.bfloat16)
        start(*k_copy(role, d))

    for role in both:
        pass_keys(role, 3)
    send_both(7)
    for role in both:
        far_product(role, 1)
    for role in both:
        far_total(role, 1)
    send_both(8)

    soon, late = pl.ds(0, 2 * TOK), pl.ds(2 * TOK, 2 * TOK)

    def own_late(role):
        arrived(x_copy(OWN, role, 3, None))
        arrived(x_copy(OWN, role, 2, None))
        g[OWN, role] = dot_rows(xs[OWN, role, late, :], dks[role, late, :])

    def own_soon(role):
        g[OWN, role] += dot_rows(xs[OWN, role, soon, :], dks[role, soon, :])
        start(*g_core(OWN, role))

    def own_total(role):
        arrived(g_core(OWN, role))
        arrived((gzs.at[role], gzr.at[role], GZ0 + role, at(dzh=1)))
        return g[OWN, role, mine, :] + gcore[OWN, role] + gzr[role].astype(jnp.float32)

    own_keys = keys_part(LEFT, 0) + keys_part(RIGHT, 0)
    part[...] = own_keys
    pass_keys(LEFT, 2)
    own_late(RIGHT)
    send_both(9)
    arrived(x_copy(OWN, RIGHT, 1, None))
    own_soon(RIGHT)
    pass_keys(RIGHT, 2)
    own_late(LEFT)
    gys[...] = own_total(RIGHT).astype(jnp.bfloat16)
    start(gys, gyr, GY, at(dy=-1))
    pass_keys(RIGHT, 1)
    pass_keys(LEFT, 1)
    own_soon(LEFT)

    for k in (1, 2, 3):
        came = pl.ds(pl.multiple_of(((x + 4 - k) % 4) * 32, 32), 32)
        arrived((pseudo.at[came], pseudo.at[came], FB0 + k - 1, at(dx=k)))
    new_mom = 0.9 * mom_ref[...] + pseudo[...]
    new_mom_ref[...] = new_mom
    new_outer_ref[...] = outer_ref[...] - 0.7 * (pseudo[...] + 0.9 * new_mom)

    g[OWN, LEFT, mine, :] = own_total(LEFT)

    own_keys = part[...]
    for role in both:
        arrived(k_copy(role, 1))
        own_keys = own_keys + krecv[role, 0].astype(jnp.float32)
    keys_ref[...] = own_keys.astype(jnp.bfloat16)

    arrived((gys, gyr, GY, at(dy=-1)))
    grad_ref[...] = g[OWN, LEFT, mine, :] + gyr[...].astype(jnp.float32)

    for role in both:
        copy(*g_core(FAR, role)).wait_send()
        copy(gzs.at[role], gzr.at[role], GZ0 + role, at(dzh=1)).wait_send()
    for moved in started:
        if id(moved) not in left:
            moved.wait_send()


def finish(*refs):
    moves = [pltpu.make_async_copy(refs[k], refs[4 + k], refs[8].at[k]) for k in range(4)]
    for move in moves:
        move.start()
    for move in moves:
        move.wait()


def body(key_grad, layer_input, key_weight, outer_frag, momentum, inner_frag):
    held = (key_grad, layer_input, key_weight, outer_frag, momentum, inner_frag)
    held = [pltpu.with_memory_space_constraint(a, pltpu.HBM) for a in held]
    whole = pl.BlockSpec(memory_space=pltpu.VMEM)
    bf16, f32 = jnp.bfloat16, jnp.float32
    results = pl.pallas_call(
        kernel,
        name="exchange",
        out_shape=(
            jax.ShapeDtypeStruct((TOK, FEAT), bf16),
            jax.ShapeDtypeStruct((ROWS, FEAT), f32),
            jax.ShapeDtypeStruct(outer_frag.shape, f32),
            jax.ShapeDtypeStruct(outer_frag.shape, f32),
        ),
        in_specs=[pl.BlockSpec(memory_space=pl.ANY)] * 6,
        out_specs=(whole,) * 4,
        scratch_shapes=[
            pltpu.VMEM((2, 2, 4 * TOK, 512), bf16),
            pltpu.VMEM((2, 4 * TOK, FEAT), bf16),
            pltpu.VMEM((2, 2, 2 * ROWS, FEAT), bf16),
            pltpu.VMEM((TOK, FEAT), f32),
            pltpu.VMEM((2, 3, TOK, FEAT), bf16),
            pltpu.VMEM((2, 3, TOK, FEAT), bf16),
            pltpu.VMEM((2, 2, 2 * ROWS, FEAT), f32),
            pltpu.VMEM((2, 2, ROWS, FEAT), f32),
            pltpu.VMEM((2, ROWS, FEAT), bf16),
            pltpu.VMEM((2, ROWS, FEAT), bf16),
            pltpu.VMEM((ROWS, FEAT), bf16),
            pltpu.VMEM((ROWS, FEAT), bf16),
            pltpu.VMEM((128, 256), f32),
            pltpu.VMEM((128, 256), f32),
            pltpu.VMEM((128, 256), bf16),
            pltpu.VMEM((3, 32, 256), bf16),
            pltpu.VMEM((32, 256), f32),
            pltpu.VMEM((3, 8, 256), f32),
            pltpu.VMEM((128, 256), f32),
            pltpu.SemaphoreType.DMA((COPIES,)),
            pltpu.SemaphoreType.DMA((COPIES,)),
            pltpu.SemaphoreType.DMA((10,)),
            pltpu.SemaphoreType.REGULAR((2,)),
        ],
        compiler_params=pltpu.CompilerParams(
            collective_id=0, has_side_effects=True, vmem_limit_bytes=VMEM_MB << 20
        ),
    )(*held)
    keys, grad, new_outer, new_momentum = pl.pallas_call(
        finish,
        name="finish",
        out_shape=[jax.ShapeDtypeStruct(r.shape, r.dtype) for r in results],
        in_specs=[whole] * 4,
        out_specs=[pl.BlockSpec(memory_space=pl.ANY)] * 4,
        scratch_shapes=[pltpu.SemaphoreType.DMA((4,))],
        compiler_params=pltpu.CompilerParams(vmem_limit_bytes=FINISH_KB << 10),
    )(*results)
    return keys, grad[None], new_outer, new_momentum


def solution(mesh):
    placed = (
        P(("island", "fsdp"), None),
        P(("island", "fsdp"), None),
        P("island", "fsdp", None),
        P(None, "fsdp"),
        P(None, "fsdp"),
        P("island", "fsdp"),
    )
    return jax.shard_map(
        body,
        mesh=mesh,
        in_specs=placed,
        out_specs=(
            P(("island", "fsdp"), None),
            P("island", "fsdp", None),
            P(None, "fsdp"),
            P(None, "fsdp"),
        ),
        check_vma=False,
    )
```

```python
import functools

import jax
import jax.numpy as jnp
from jax import lax
from jax.experimental import pallas as pl
from jax.experimental.pallas import tpu as pltpu
from jax.sharding import PartitionSpec as P

MESH = pl.DeviceIdType.MESH
TOK, WIDTH, FEAT, ROWS = 128, 8192, 512, 256
LEFT, RIGHT = 0, 1
FAR, OWN = 0, 1
VMEM_MB = 40
FINISH_KB = 53248
PLAN = ((1, 1, 1, 1, 1, 1, 1, 1, 1, 1), (1, 1, 1, 1, 1, 1, 1, 1, 1, 1))
DEPTH = (2, 2)
ORDER = ('a3', 'a2', 'a1', 'o3', 'b3', 'b2', 'b1', 'o2', 'o1')

X0 = 0
DK0 = X0 + 18
WY = DK0 + 6
WC0 = WY + 1
WZ0 = WC0 + 4
GC0 = WZ0 + 2
GZ0 = GC0 + 4
GY = GZ0 + 2
K0 = GY + 1
FX0 = K0 + 6
FZ0 = FX0 + 3
FA0 = FZ0 + 3
FB0 = FA0 + 3
COPIES = FB0 + 3


def dot(a, b):
    return jnp.dot(a, b, preferred_element_type=jnp.float32)


def dot_rows(a, b):
    return lax.dot_general(a, b, (((0,), (0,)), ((), ())), preferred_element_type=jnp.float32)


def kernel(
    dk_ref, x_ref, w_ref, outer_hbm, mom_hbm, inner_hbm,
    keys_ref, grad_ref, new_outer_ref, new_mom_ref,
    xs, dks, ws, part, ksend, krecv, g, gcore, gzs, gzr, gys, gyr,
    outer_ref, mom_ref, inner_ref, fx, acc, fz, pseudo, send, recv, local, entered,
):
    island, f = lax.axis_index("island"), lax.axis_index("fsdp")
    x, zl = island // 4, island % 4
    zh, y, c = f // 16, (f // 2) % 8, f % 2

    def at(dx=0, dzl=0, dzh=0, dy=0, dc=0):
        return (
            ((x + dx) % 4) * 4 + (zl + dzl) % 4,
            ((zh + dzh) % 2) * 16 + ((y + dy + 8) % 8) * 2 + (c + dc) % 2,
        )

    def copy(src, dst, sem, to):
        return pltpu.make_async_remote_copy(
            src_ref=src, dst_ref=dst, send_sem=send.at[sem], recv_sem=recv.at[sem],
            device_id=to, device_id_type=MESH,
        )

    started = []

    def start(src, dst, sem, to):
        moved = copy(src, dst, sem, to)
        moved.start()
        started.append(moved)
        return moved

    def cols(owner, plane, h=None):
        first = ((plane + 2) % 2) * 4096 + ((owner + 8) % 8) * 512
        if h is None:
            return pl.ds(pl.multiple_of(first, 512), 512)
        return pl.ds(pl.multiple_of(first + h * 256, 256), 256)

    def part_cols(h):
        return pl.ds(0, 512) if h is None else pl.ds(h * 256, 256)

    def tok(d):
        return pl.ds(d * TOK, TOK)

    mine = pl.ds(pl.multiple_of(c * ROWS, ROWS), ROWS)
    other = pl.ds(pl.multiple_of((1 - c) * ROWS, ROWS), ROWS)
    plane = [zh + 1, zh]

    loads = []
    for role in (LEFT, RIGHT):
        loads.append((dk_ref, dks.at[role, tok(0)]))
        for p in (FAR, OWN):
            loads.append((x_ref.at[:, cols(y - role, plane[p])], xs.at[p, role, tok(0)]))
    loads.append((w_ref.at[0], ws.at[OWN, LEFT, mine]))
    loads += [(inner_hbm, inner_ref), (outer_hbm, outer_ref), (mom_hbm, mom_ref)]
    loads = [pltpu.make_async_copy(s, d, local.at[k]) for k, (s, d) in enumerate(loads)]
    for load in loads:
        load.start()

    barrier = pltpu.get_barrier_semaphore()

    def tell(semaphore, partner):
        pl.semaphore_signal(semaphore, inc=1, device_id=partner, device_id_type=MESH)

    level = [at(dy=d) for d in (1, -1, 2, -2, 3, -3)] + [at(dc=1)] + [at(dx=k) for k in (1, 2, 3)]
    upright = [(at(dzh=1), zh == 0)] + [(at(dzl=k), zl + k < 4) for k in (1, 2, 3)]
    for partner in level:
        tell(barrier, partner)
    for partner, is_higher in upright:
        pl.when(is_higher)(functools.partial(tell, barrier, partner))
    pl.semaphore_wait(barrier, len(level) + zh + zl)
    for partner, is_higher in upright:
        pl.when(jnp.logical_not(is_higher))(functools.partial(tell, entered.at[0 if partner is upright[0][0] else 1], partner))

    sign = (1, -1)

    def x_copy(p, role, d, h):
        owner = y + d if role == LEFT else y - d - 1
        return (
            x_ref.at[:, cols(owner, plane[p], h)], xs.at[p, role, tok(d), part_cols(h)],
            X0 + (2 * p + (h or 0)) * 6 + role * 3 + d - 1, at(dy=sign[role] * d),
        )

    def dk_copy(role, d):
        src = dk_ref if d == 1 else dks.at[role, tok(d - 1)]
        return src, dks.at[role, tok(d)], DK0 + role * 3 + d - 1, at(dy=sign[role])

    def w_core(p, role):
        src = w_ref.at[0] if (p, role) == (OWN, LEFT) else ws.at[p, role, mine]
        return src, ws.at[p, role, mine], WC0 + p * 2 + role, at(dc=1)

    def w_far(role):
        src = w_ref.at[0] if role == LEFT else ws.at[OWN, role, mine]
        return src, ws.at[FAR, role, mine], WZ0 + role, at(dzh=1)

    w_next = (w_ref.at[0], ws.at[OWN, RIGHT, mine], WY, at(dy=1))

    def k_copy(role, d):
        return ksend.at[role, d - 1], krecv.at[role, d - 1], K0 + role * 3 + d - 1, at(dy=-sign[role])

    seen = set()

    def arrived(args):
        if args[2] not in seen:
            seen.add(args[2])
            copy(*args).wait_recv()

    kinds = {"a": (FAR, 0), "b": (FAR, 1), "o": (OWN, None)}
    order = [(kinds[e[0]][0], int(e[1]), kinds[e[0]][1]) for e in ORDER]
    under_way, left = ([], []), []
    both = (RIGHT, LEFT)

    def send_x(role):
        sent, depth = under_way[role], DEPTH[role]
        if len(sent) == len(order):
            return
        if len(sent) >= depth:
            sent[-depth].wait_send()
            left.append(id(sent[-depth]))
        p, d, h = order[len(sent)]
        sent.append(start(*x_copy(p, role, d, h)))

    def send_both(site):
        for role in both:
            for _ in range(PLAN[role][site]):
                send_x(role)

    for role in both:
        start(*dk_copy(role, 1))
    start(*w_next)
    first_far = copy(*w_far(LEFT))
    started.append(first_far)
    pl.when(zh == 1)(first_far.start)
    start(*w_core(OWN, LEFT))
    for k in (1, 2, 3):
        peer = (x + k) % 4
        start(inner_hbm.at[pl.ds(pl.multiple_of(peer * 32, 32), 32)], fx.at[k - 1], FX0 + k - 1, at(dx=k))
    send_both(0)

    for role in both:
        arrived(dk_copy(role, 1))
        start(*dk_copy(role, 2))
    send_both(1)

    @pl.when(zh == 0)
    def _():
        pl.semaphore_wait(entered.at[0], 1)
        first_far.start()

    arrived(w_next)
    start(*w_far(RIGHT))
    start(*w_core(OWN, RIGHT))
    for role in both:
        arrived(dk_copy(role, 2))
        start(*dk_copy(role, 3))
    send_both(2)

    for load in loads:
        load.wait()

    block = pl.ds(pl.multiple_of(x * 32, 32), 32)
    eight = pl.ds(pl.multiple_of(x * 32 + zl * 8, 8), 8)
    outer_block = outer_ref[block, :]
    total = outer_block - inner_ref[block, :].astype(jnp.float32)
    for k in (1, 2, 3):
        arrived((fx.at[k - 1], fx.at[k - 1], FX0 + k - 1, at(dx=k)))
        total = total + (outer_block - fx[k - 1].astype(jnp.float32))
    acc[...] = total

    @pl.when(zl < 3)
    def _():
        pl.semaphore_wait(entered.at[1], 3 - zl)

    for k in (1, 2, 3):
        peer = (zl + k) % 4
        start(acc.at[pl.ds(pl.multiple_of(peer * 8, 8), 8)], fz.at[k - 1], FZ0 + k - 1, at(dzl=k))

    send_both(3)

    total = acc[pl.ds(pl.multiple_of(zl * 8, 8), 8), :]
    for k in (1, 2, 3):
        arrived((fz.at[k - 1], fz.at[k - 1], FZ0 + k - 1, at(dzl=k)))
        total = total + fz[k - 1]
    pseudo[eight, :] = total / 16
    for k in (1, 2, 3):
        start(pseudo.at[eight], pseudo.at[eight], FA0 + k - 1, at(dzl=k))

    arrived(w_far(LEFT))
    start(*w_core(FAR, LEFT))

    send_both(4)

    def g_core(p, role):
        return g.at[p, role, other], gcore.at[p, role], GC0 + p * 2 + role, at(dc=1)

    def far_product(role, h):
        for d in (3, 2, 1):
            arrived(x_copy(FAR, role, d, h))
        if h == 0:
            arrived(dk_copy(role, 3))
        g[FAR, role, pl.ds(h * 256, 256), :] = dot_rows(xs[FAR, role, :, part_cols(h)], dks[role])
        moved = copy(*g_core(FAR, role))
        pl.when(c != h)(moved.start)

    def far_total(role, h):
        came = copy(*g_core(FAR, role))
        moved = copy(gzs.at[role], gzr.at[role], GZ0 + role, at(dzh=1))

        @pl.when(c == h)
        def _():
            came.wait_recv()
            gzs[role] = (g[FAR, role, pl.ds(h * 256, 256), :] + gcore[FAR, role]).astype(jnp.bfloat16)
            moved.start()

    for role in both:
        far_product(role, 0)
    for role in both:
        far_total(role, 0)
    send_both(5)

    for k in (1, 2, 3):
        came = pl.ds(pl.multiple_of(x * 32 + ((zl + 4 - k) % 4) * 8, 8), 8)
        arrived((pseudo.at[came], pseudo.at[came], FA0 + k - 1, at(dzl=k)))
    for k in (1, 2, 3):
        start(pseudo.at[block], pseudo.at[block], FB0 + k - 1, at(dx=k))
    arrived(w_far(RIGHT))
    start(*w_core(FAR, RIGHT))

    send_both(6)
    for role in both:
        for p in (FAR, OWN):
            arrived(w_core(p, role))

    def keys_part(role, d):
        return dot(xs[FAR, role, tok(d), :], ws[FAR, role]) + dot(xs[OWN, role, tok(d), :], ws[OWN, role])

    def pass_keys(role, d):
        arrived(x_copy(FAR, role, d, 0))
        arrived(x_copy(FAR, role, d, 1))
        arrived(x_copy(OWN, role, d, None))
        value = keys_part(role, d)
        if d < 3:
            arrived(k_copy(role, d + 1))
            value = value + krecv[role, d].astype(jnp.float32)
        ksend[role, d - 1] = value.astype(jnp.bfloat16)
        start(*k_copy(role, d))

    for role in both:
        pass_keys(role, 3)
    send_both(7)
    for role in both:
        far_product(role, 1)
    for role in both:
        far_total(role, 1)
    send_both(8)

    soon, late = pl.ds(0, 2 * TOK), pl.ds(2 * TOK, 2 * TOK)

    def own_late(role):
        arrived(x_copy(OWN, role, 3, None))
        arrived(x_copy(OWN, role, 2, None))
        g[OWN, role] = dot_rows(xs[OWN, role, late, :], dks[role, late, :])

    def own_soon(role):
        g[OWN, role] += dot_rows(xs[OWN, role, soon, :], dks[role, soon, :])
        start(*g_core(OWN, role))

    def own_total(role):
        arrived(g_core(OWN, role))
        arrived((gzs.at[role], gzr.at[role], GZ0 + role, at(dzh=1)))
        return g[OWN, role, mine, :] + gcore[OWN, role] + gzr[role].astype(jnp.float32)

    pass_keys(LEFT, 2)
    pass_keys(RIGHT, 2)
    own_keys = keys_part(LEFT, 0) + keys_part(RIGHT, 0)
    part[...] = own_keys
    own_late(RIGHT)
    send_both(9)
    arrived(x_copy(OWN, RIGHT, 1, None))
    own_soon(RIGHT)
    own_late(LEFT)
    gys[...] = own_total(RIGHT).astype(jnp.bfloat16)
    start(gys, gyr, GY, at(dy=-1))
    pass_keys(LEFT, 1)
    own_soon(LEFT)
    pass_keys(RIGHT, 1)

    for k in (1, 2, 3):
        came = pl.ds(pl.multiple_of(((x + 4 - k) % 4) * 32, 32), 32)
        arrived((pseudo.at[came], pseudo.at[came], FB0 + k - 1, at(dx=k)))
    new_mom = 0.9 * mom_ref[...] + pseudo[...]
    new_mom_ref[...] = new_mom
    new_outer_ref[...] = outer_ref[...] - 0.7 * (pseudo[...] + 0.9 * new_mom)

    g[OWN, LEFT, mine, :] = own_total(LEFT)

    own_keys = part[...]
    for role in both:
        arrived(k_copy(role, 1))
        own_keys = own_keys + krecv[role, 0].astype(jnp.float32)
    keys_ref[...] = own_keys.astype(jnp.bfloat16)

    arrived((gys, gyr, GY, at(dy=-1)))
    grad_ref[...] = g[OWN, LEFT, mine, :] + gyr[...].astype(jnp.float32)

    for role in both:
        copy(*g_core(FAR, role)).wait_send()
        copy(gzs.at[role], gzr.at[role], GZ0 + role, at(dzh=1)).wait_send()
    for moved in started:
        if id(moved) not in left:
            moved.wait_send()


def finish(*refs):
    moves = [pltpu.make_async_copy(refs[k], refs[4 + k], refs[8].at[k]) for k in range(4)]
    for move in moves:
        move.start()
    for move in moves:
        move.wait()


def body(key_grad, layer_input, key_weight, outer_frag, momentum, inner_frag):
    held = (key_grad, layer_input, key_weight, outer_frag, momentum, inner_frag)
    held = [pltpu.with_memory_space_constraint(a, pltpu.HBM) for a in held]
    whole = pl.BlockSpec(memory_space=pltpu.VMEM)
    bf16, f32 = jnp.bfloat16, jnp.float32
    results = pl.pallas_call(
        kernel,
        name="exchange",
        out_shape=(
            jax.ShapeDtypeStruct((TOK, FEAT), bf16),
            jax.ShapeDtypeStruct((ROWS, FEAT), f32),
            jax.ShapeDtypeStruct(outer_frag.shape, f32),
            jax.ShapeDtypeStruct(outer_frag.shape, f32),
        ),
        in_specs=[pl.BlockSpec(memory_space=pl.ANY)] * 6,
        out_specs=(whole,) * 4,
        scratch_shapes=[
            pltpu.VMEM((2, 2, 4 * TOK, 512), bf16),
            pltpu.VMEM((2, 4 * TOK, FEAT), bf16),
            pltpu.VMEM((2, 2, 2 * ROWS, FEAT), bf16),
            pltpu.VMEM((TOK, FEAT), f32),
            pltpu.VMEM((2, 3, TOK, FEAT), bf16),
            pltpu.VMEM((2, 3, TOK, FEAT), bf16),
            pltpu.VMEM((2, 2, 2 * ROWS, FEAT), f32),
            pltpu.VMEM((2, 2, ROWS, FEAT), f32),
            pltpu.VMEM((2, ROWS, FEAT), bf16),
            pltpu.VMEM((2, ROWS, FEAT), bf16),
            pltpu.VMEM((ROWS, FEAT), bf16),
            pltpu.VMEM((ROWS, FEAT), bf16),
            pltpu.VMEM((128, 256), f32),
            pltpu.VMEM((128, 256), f32),
            pltpu.VMEM((128, 256), bf16),
            pltpu.VMEM((3, 32, 256), bf16),
            pltpu.VMEM((32, 256), f32),
            pltpu.VMEM((3, 8, 256), f32),
            pltpu.VMEM((128, 256), f32),
            pltpu.SemaphoreType.DMA((COPIES,)),
            pltpu.SemaphoreType.DMA((COPIES,)),
            pltpu.SemaphoreType.DMA((10,)),
            pltpu.SemaphoreType.REGULAR((2,)),
        ],
        compiler_params=pltpu.CompilerParams(
            collective_id=0, has_side_effects=True, vmem_limit_bytes=VMEM_MB << 20
        ),
    )(*held)
    keys, grad, new_outer, new_momentum = pl.pallas_call(
        finish,
        name="finish",
        out_shape=[jax.ShapeDtypeStruct(r.shape, r.dtype) for r in results],
        in_specs=[whole] * 4,
        out_specs=[pl.BlockSpec(memory_space=pl.ANY)] * 4,
        scratch_shapes=[pltpu.SemaphoreType.DMA((4,))],
        compiler_params=pltpu.CompilerParams(vmem_limit_bytes=FINISH_KB << 10),
    )(*results)
    return keys, grad[None], new_outer, new_momentum


def solution(mesh):
    placed = (
        P(("island", "fsdp"), None),
        P(("island", "fsdp"), None),
        P("island", "fsdp", None),
        P(None, "fsdp"),
        P(None, "fsdp"),
        P("island", "fsdp"),
    )
    return jax.shard_map(
        body,
        mesh=mesh,
        in_specs=placed,
        out_specs=(
            P(("island", "fsdp"), None),
            P("island", "fsdp", None),
            P(None, "fsdp"),
            P(None, "fsdp"),
        ),
        check_vma=False,
    )
```
